128 devices in a mesh: seq: 16 (over z_hi, y, core), kv: 8 (over x, z_lo).
Axes of the slice: x: 4, y: 4, z: 4 (z_hi: 2, z_lo: 2; z = z_hi * 2 + z_lo), core: 2. Of those that a mesh axis runs over, the one named last changes fastest.
Arguments:
- queries: bfloat16 [16384, 4096], P('seq', 'kv'), may hold values from -100 to 100
- resp_keys: bfloat16 [16384, 1024], P('seq', 'kv'), may hold values from -6 to 6
- resp_values: bfloat16 [16384, 1024], P('seq', 'kv'), may hold values from -6 to 6
- prompt_keys: bfloat16 [16384, 1024], P('seq', 'kv'), may hold values from -6 to 6
- prompt_values: bfloat16 [16384, 1024], P('seq', 'kv'), may hold values from -6 to 6
- out_weight: bfloat16 [4096, 4096], P('kv'), may hold values from -0.125 to 0.125
- grad_out: bfloat16 [16384, 4096], P('seq', 'kv'), may hold values from -6 to 6
- response_group: int32 [256, 1], P('seq'), may hold values from 0 to 15
- prompt_len: int32 [16], replicated, may hold values from 256 to 1024, as said below
Outputs:
- layer_out: bfloat16 [16384, 4096], P('seq', 'kv')
- query_grad: bfloat16 [16384, 4096], P('seq', 'kv')
- key_grad: bfloat16 [16384, 1024], P('seq', 'kv')
- value_grad: bfloat16 [16384, 1024], P('seq', 'kv')
- prompt_key_grad: bfloat16 [16384, 1024], P('seq', 'kv')
- prompt_value_grad: bfloat16 [16384, 1024], P('seq', 'kv')
The draws below stay inside these ranges and needn't reach their ends.
Inputs may be any that keep to these rules, and one draw needn't show every extreme that they name: `prompt_len`: at least one group has all 1024 prompt tokens live. `response_group`: every group has at least one response.
All inputs are finite; a program needn't handle non-finite values.
Results may differ from the reference program's by a relative error of at most 0.04.
Values may be sent and summed in bfloat16 or wider, within the bound.
No kernel may reach another device: no remote copies, remote signals or barrier semaphores. Data moves between devices by JAX's collectives and lax.ppermute only.
A program may use at most 192 MiB of HBM per device.

```python
import jax
import jax.numpy as jnp
from jax import lax

D = 4096
HD = 128
QPK = 4
PL = 1024
RL = 64
R_DEV = 16
KVH = 8
QH = 32
NG = 16
BLOCKS = 256
TOK = 16384
N_SEQ = 16


def shared_keys(key):
    return jnp.clip(jax.random.normal(key, (TOK, KVH * HD), jnp.float32), -6.0, 6.0)


def draw_resp_keys(key, part):
    base = shared_keys(key)
    return base.astype(jnp.bfloat16)


def draw_queries(key, part):
    key = jax.random.fold_in(key, 11)
    drawn = jnp.clip(jax.random.normal(key, (TOK, QH * HD), jnp.float32), -6.0, 6.0)
    return drawn.astype(jnp.bfloat16)


def draw_prompt_len(key, part):
    key = jax.random.fold_in(key, 7)
    lengths = jax.random.randint(key, (NG,), PL // 4, PL + 1)
    picked = jax.random.randint(jax.random.fold_in(key, 1), (), 0, NG)
    return jnp.where(jnp.arange(NG) == picked, PL, lengths).astype(jnp.int32)


def raised(array, rng, source, target, blocks, factor):
    def block_of(dim):
        return (jnp.arange(array.shape[dim]) // (array.shape[dim] // blocks)).reshape((-1,) + (1,) * (array.ndim - 1 - dim))

    one_side = jax.random.permutation(rng, blocks)[block_of(target)]
    other_side = (block_of(target) + blocks // 2) % blocks
    return jnp.where((block_of(source) == one_side) | (block_of(source) == other_side), factor * array, array)


def block_scale(own_key, dims, shards, low, largest):
    gain, own = 1.0, jax.random.fold_in(own_key, 6)
    for dim, parts in shards:
        steps = jnp.exp(jax.random.uniform(jax.random.fold_in(own, dim), (parts,), jnp.float32, low / len(shards), largest / len(shards)))
        gain = gain * jnp.repeat(steps, dims[dim] // parts).reshape([-1 if axis == dim else 1 for axis in range(len(dims))])
    return gain


def choose_distinct(rng, rows, count, top, lift):
    sequence = jax.random.permutation(jax.random.fold_in(rng, 1), count)
    pull = sequence
    for power in range(3):
        pull = pull * pull // count
    pull = pull * lift // count
    lots = jax.random.randint(jax.random.fold_in(rng, 2), (rows, count), 0, 4096) + pull
    sure = jax.random.permutation(jax.random.fold_in(rng, 3), rows)[jnp.arange(count) % rows]
    lots = jnp.where(jnp.arange(rows)[:, None] == sure[None, :], 1 << 14, lots)
    score = lots * count + jnp.arange(count)
    return lax.top_k(score.astype(jnp.int32), top)[1].astype(jnp.int32)


def scatter_about(rng, extent, scale, bound, cuts=(), held_as=jnp.bfloat16):
    loudness = block_scale(rng, extent, cuts, -0.22, 0.18) if cuts else 1.0
    entries = jax.random.normal(rng, extent, jnp.float32) * scale * loudness
    return jnp.minimum(jnp.maximum(entries, -bound), bound).astype(held_as)


def gaussian_with(own_key, shape, width, most, cuts, heavy, held_as=jnp.bfloat16):
    values = width * jax.random.normal(own_key, shape, jnp.float32)
    if cuts:
        values = values * block_scale(own_key, shape, cuts, -0.22, 0.18)
    return jnp.clip(raised(values, jax.random.fold_in(own_key, 3), *heavy), -most, most).astype(held_as)


def setup_inputs(seed: int = 0) -> dict:
    splits = jax.random.split(jax.random.key(seed), 10)
    queries = draw_queries(jax.random.fold_in(splits[9], 71), 0)
    resp_keys = draw_resp_keys(jax.random.fold_in(splits[9], 71), 0)
    resp_values = scatter_about(splits[2], (TOK, KVH * HD), 1.0, 6.0, ((0, 16), (1, 8)))
    prompt_keys = scatter_about(splits[3], (NG * PL, KVH * HD), 1.0, 6.0, ((0, 16), (1, 8)))
    prompt_values = scatter_about(splits[4], (NG * PL, KVH * HD), 1.0, 6.0, ((0, 16), (1, 8)))
    out_weight = gaussian_with(splits[5], (QH * HD, D), (QH * HD) ** -0.5, 0.125, ((0, 8),), (0, 1, 8, 2.0))
    grad_out = scatter_about(splits[6], (TOK, D), 1.0, 6.0, ((0, 16), (1, 8)))
    response_group = choose_distinct(splits[7], BLOCKS, NG, 1, 512)
    prompt_len = draw_prompt_len(jax.random.fold_in(splits[9], 71), 0)
    return {"queries": queries, "resp_keys": resp_keys, "resp_values": resp_values, "prompt_keys": prompt_keys, "prompt_values": prompt_values, "out_weight": out_weight, "grad_out": grad_out, "response_group": response_group, "prompt_len": prompt_len}


def reference(queries, resp_keys, resp_values, prompt_keys, prompt_values, out_weight, grad_out, response_group, prompt_len):
    f32 = jnp.float32
    score_scale = HD ** -0.5
    query_all = queries.reshape(N_SEQ, R_DEV, RL, KVH, QPK, HD)
    keys_all = resp_keys.reshape(N_SEQ, R_DEV, RL, KVH, HD)
    values_all = resp_values.reshape(N_SEQ, R_DEV, RL, KVH, HD)
    prompt_k = prompt_keys.reshape(NG, PL, KVH, HD)
    prompt_v = prompt_values.reshape(NG, PL, KVH, HD)
    cotangent = grad_out.reshape(N_SEQ, R_DEV * RL, D)
    group_ids = response_group.reshape(N_SEQ, R_DEV).astype(jnp.int32)
    weight_heads = out_weight.reshape(KVH, QPK * HD, D).astype(f32)

    def device_step(totals, slices):
        grad_pk, grad_pv = totals
        query_blk, own_keys, own_values, out_grad, groups = slices
        member = groups[:, None] == jnp.arange(NG, dtype=jnp.int32)[None, :]
        prompt_live = jnp.sum(jnp.where(member, prompt_len[None, :], 0), axis=1)
        all_keys = jnp.concatenate([prompt_k[groups], own_keys], axis=1)
        all_values = jnp.concatenate([prompt_v[groups], own_values], axis=1)
        scores = jnp.einsum('rihgd,rjhd->rhgij', query_blk.astype(f32), all_keys.astype(f32)) * score_scale
        key_pos = jnp.arange(PL + RL)[None, None, :]
        query_pos = jnp.arange(RL)[None, :, None]
        visible = jnp.where(key_pos < PL, key_pos < prompt_live[:, None, None], key_pos - PL <= query_pos)
        scores = jnp.where(visible[:, None, None], scores, -jnp.inf)
        row_max = jnp.max(scores, axis=-1, keepdims=True)
        expo = jnp.exp(scores - row_max)
        weights = expo / jnp.sum(expo, axis=-1, keepdims=True)
        weights_bf = weights.astype(jnp.bfloat16)
        attended = jnp.einsum('rhgij,rjhd->rihgd', weights_bf.astype(f32), all_values.astype(f32)).astype(jnp.bfloat16)
        attended_rows = attended.reshape(R_DEV * RL, KVH, QPK * HD).astype(f32)
        head_parts = jnp.einsum('thc,hcn->htn', attended_rows, weight_heads)
        head_parts = lax.optimization_barrier(head_parts.astype(jnp.bfloat16))
        layer_rows = jnp.sum(head_parts.astype(f32), axis=0).astype(jnp.bfloat16)
        attended_grad = jnp.dot(out_grad, out_weight.T, preferred_element_type=f32).astype(jnp.bfloat16)
        attended_grad = attended_grad.reshape(R_DEV, RL, KVH, QPK, HD)
        grad_values = jnp.einsum('rhgij,rihgd->rjhd', weights_bf.astype(f32), attended_grad.astype(f32))
        prob_grad = jnp.einsum('rihgd,rjhd->rhgij', attended_grad.astype(f32), all_values.astype(f32))
        row_dot = jnp.sum(attended_grad.astype(f32) * attended.astype(f32), axis=-1)
        row_dot = jnp.transpose(row_dot, (0, 2, 3, 1))[..., None]
        score_grad = (weights * (prob_grad - row_dot)).astype(jnp.bfloat16)
        query_grad = (jnp.einsum('rhgij,rjhd->rihgd', score_grad.astype(f32), all_keys.astype(f32)) * score_scale).astype(jnp.bfloat16)
        grad_keys = jnp.einsum('rhgij,rihgd->rjhd', score_grad.astype(f32), query_blk.astype(f32)) * score_scale
        member_f = member.astype(f32)
        part_k = jnp.einsum('rg,rphd->gphd', member_f, grad_keys[:, :PL], precision=lax.Precision.HIGHEST)
        part_v = jnp.einsum('rg,rphd->gphd', member_f, grad_values[:, :PL], precision=lax.Precision.HIGHEST)
        part_k = lax.optimization_barrier(part_k.astype(jnp.bfloat16))
        part_v = lax.optimization_barrier(part_v.astype(jnp.bfloat16))
        grad_pk = grad_pk + part_k.astype(f32)
        grad_pv = grad_pv + part_v.astype(f32)
        outs = (layer_rows, query_grad, grad_keys[:, PL:].astype(jnp.bfloat16), grad_values[:, PL:].astype(jnp.bfloat16))
        return (grad_pk, grad_pv), outs

    zeros_init = jnp.zeros((NG, PL, KVH, HD), f32)
    totals, stacked = lax.scan(device_step, (zeros_init, zeros_init), (query_all, keys_all, values_all, cotangent, group_ids))
    layer_out = stacked[0].reshape(TOK, D)
    query_grad = stacked[1].reshape(TOK, QH * HD)
    key_grad = stacked[2].reshape(TOK, KVH * HD)
    value_grad = stacked[3].reshape(TOK, KVH * HD)
    prompt_key_grad = totals[0].reshape(NG * PL, KVH * HD).astype(jnp.bfloat16)
    prompt_value_grad = totals[1].reshape(NG * PL, KVH * HD).astype(jnp.bfloat16)
    return (layer_out, query_grad, key_grad, value_grad, prompt_key_grad, prompt_value_grad)
```

```python
import functools
import math

import jax
import jax.numpy as jnp
from jax import lax
from jax.experimental import pallas as pl
from jax.experimental.pallas import tpu as pltpu
from jax.sharding import PartitionSpec as P

HD = 128
QPK = 4
PL = 1024
RL = 64
ROWS = QPK * RL
TILE = 256
NT = PL // TILE
HALF = 8
SCALE = HD ** (-0.5)
LOG2E = math.log2(math.e)
C2 = SCALE * LOG2E
MIB = 1024 * 1024
F32 = jnp.float32
BF16 = jnp.bfloat16

A0, B0, AM, AP, BM, BP, A2, B2 = range(8)
PLACE = (A0, AP, A2, AM, B0, BP, B2, BM)
STAGES = ((A2, B2), (AM, AP, BM, BP), (A0, B0))


def kv_perm(move):
    return [
        (x * 2 + z, (move(x, z)[0] % 4) * 2 + move(x, z)[1]) for x in range(4) for z in range(2)
    ]


def seq_perm(move):
    pairs = []
    for h in range(2):
        for y in range(4):
            for c in range(2):
                h2, y2, c2 = move(h, y, c)
                pairs.append((h * 8 + y * 2 + c, h2 * 8 + (y2 % 4) * 2 + c2))
    return pairs


X_UP = kv_perm(lambda x, z: (x + 1, z))
X_DOWN = kv_perm(lambda x, z: (x - 1, z))
Z_LO = kv_perm(lambda x, z: (x, 1 - z))
Y_UP = seq_perm(lambda h, y, c: (h, y + 1, c))
Y_DOWN = seq_perm(lambda h, y, c: (h, y - 1, c))
Z_HI = seq_perm(lambda h, y, c: (1 - h, y, c))
CORE = seq_perm(lambda h, y, c: (h, y, 1 - c))


def kv_send(a, perm):
    return lax.ppermute(a, "kv", perm)


def seq_send(a, perm):
    return lax.ppermute(a, "seq", perm)


def dot_nt(a, b):
    return lax.dot_general(a, b, (((1,), (1,)), ((), ())), preferred_element_type=F32)


def dot_nn(a, b):
    return lax.dot_general(a, b, (((1,), (0,)), ((), ())), preferred_element_type=F32)


def dot_tn(a, b):
    return lax.dot_general(a, b, (((0,), (0,)), ((), ())), preferred_element_type=F32)


def stacked_heads(ref, row):
    block = ref[pl.ds(row, RL), :]
    return jnp.concatenate([block[:, h * HD : (h + 1) * HD] for h in range(QPK)], axis=0)


def spread_heads(stacked):
    return jnp.concatenate([stacked[h * RL : (h + 1) * RL] for h in range(QPK)], axis=1)


def causal_mask():
    key = lax.broadcasted_iota(jnp.int32, (RL, ROWS), 0)
    query = lax.broadcasted_iota(jnp.int32, (RL, ROWS), 1) % RL
    return key <= query


def tile_mask(tile, live):
    key = lax.broadcasted_iota(jnp.int32, (TILE, ROWS), 0) + tile * TILE
    return key < live


def start_slot(sources, slot, buf, kv_buf, sem):
    for i, (ref, off) in enumerate(sources):

        @pl.when(slot == i)
        def _(ref=ref, off=off):
            pltpu.make_async_copy(ref.at[pl.ds(off, PL)], kv_buf.at[buf], sem.at[buf]).start()


def wait_slot(sources, buf, kv_buf, sem):
    ref, off = sources[0]
    pltpu.make_async_copy(ref.at[pl.ds(off, PL)], kv_buf.at[buf], sem.at[buf]).wait()


def fwd_kernel(count, offsets, slots, lives, q_ref, k_ref, v_ref, *rest):
    n_kv = max(i for i, _ in offsets) + 1
    kv_refs = rest[:n_kv]
    att_ref, lse_ref, kv_buf, sem = rest[n_kv:]
    sources = [(kv_refs[i], off) for i, off in offsets]
    start_slot(sources, slots[0], 0, kv_buf, sem)

    def one(r, carry):
        buf = lax.rem(r, 2)

        @pl.when(r + 1 < count)
        def _():
            start_slot(sources, slots[r + 1], 1 - buf, kv_buf, sem)

        row = pl.multiple_of(r * RL, RL)
        wait_slot(sources, buf, kv_buf, sem)
        live = lives[r]
        tiles = (live + TILE - 1) // TILE

        def work(n):
            q = stacked_heads(q_ref, row)
            scores = [dot_nt(kv_buf[buf, t * TILE : (t + 1) * TILE, :HD], q) for t in range(n)]
            scores[-1] = jnp.where(tile_mask(n - 1, live), scores[-1], -jnp.inf)
            own = jnp.where(causal_mask(), dot_nt(k_ref[pl.ds(row, RL), :], q), -jnp.inf)
            top = jnp.max(own, axis=0, keepdims=True)
            for s in scores:
                top = jnp.maximum(top, jnp.max(s, axis=0, keepdims=True))
            top = top * C2
            w_own = jnp.exp2(own * C2 - top)
            total = jnp.sum(w_own, axis=0, keepdims=True)
            out = dot_tn(v_ref[pl.ds(row, RL), :], w_own.astype(BF16))
            for t, s in enumerate(scores):
                w = jnp.exp2(s * C2 - top)
                total = total + jnp.sum(w, axis=0, keepdims=True)
                out = out + dot_tn(kv_buf[buf, t * TILE : (t + 1) * TILE, HD:], w.astype(BF16))
            out = out * (1.0 / total)
            att_ref[pl.ds(row, RL), :] = spread_heads(out.T.astype(BF16))
            lse_ref[pl.ds(pl.multiple_of(r * 8, 8), 8), :] = jnp.broadcast_to(
                top + jnp.log2(total), (8, ROWS)
            )

        for n in range(1, NT + 1):
            pl.when(tiles == n)(functools.partial(work, n))
        return carry

    lax.fori_loop(0, count, one, 0)


def bwd_kernel(n_slots, offsets, starts, order, lives, q_ref, k_ref, v_ref, da_ref, att_ref, lse_ref, *rest):
    n_kv = max(i for i, _ in offsets) + 1
    kv_refs = rest[:n_kv]
    dq_ref, dk_ref, dv_ref, other_ref, mine_ref, kv_buf, k_t, acc, sem = rest[n_kv:]
    sources = [(kv_refs[i], off) for i, off in offsets]
    half = n_slots // 2
    start_slot(sources, 0, 0, kv_buf, sem)

    def one_slot(slot, carry):
        buf = lax.rem(slot, 2)

        @pl.when(slot + 1 < n_slots)
        def _():
            start_slot(sources, slot + 1, 1 - buf, kv_buf, sem)

        wait_slot(sources, buf, kv_buf, sem)
        first, last = starts[slot], starts[slot + 1]
        acc[...] = jnp.zeros_like(acc)

        @pl.when(last > first)
        def _():
            k_t[...] = kv_buf[buf, :, :HD].T

        def one(p, inner):
            r = order[p]
            row = pl.multiple_of(r * RL, RL)
            live = lives[p]
            tiles = (live + TILE - 1) // TILE

            def work(n):
                q = stacked_heads(q_ref, row)
                da = stacked_heads(da_ref, row)
                prod = da.astype(F32) * stacked_heads(att_ref, row).astype(F32)
                high = prod.astype(BF16)
                low = (prod - high.astype(F32)).astype(BF16)
                ones = jnp.ones((8, HD), BF16)
                row_dot = (dot_nt(ones, high) + dot_nt(ones, low))[:1]
                lse = lse_ref[pl.ds(pl.multiple_of(r * 8, 8), 8), :][:1]
                k_own = k_ref[pl.ds(row, RL), :]
                w = jnp.exp2(dot_nt(k_own, q) * C2 - lse)
                w = jnp.where(causal_mask(), w, 0.0)
                ds = (w * (dot_nt(v_ref[pl.ds(row, RL), :], da) - row_dot)).astype(BF16)
                dk_ref[pl.ds(row, RL), :] = (dot_nn(ds, q) * SCALE).astype(BF16)
                dv_ref[pl.ds(row, RL), :] = dot_nn(w.astype(BF16), da).astype(BF16)
                dq = dot_tn(k_own, ds)
                for t in range(n):
                    span = slice(t * TILE, (t + 1) * TILE)
                    s = dot_nt(kv_buf[buf, span, :HD], q)
                    w = jnp.exp2(s * C2 - lse)
                    if t == n - 1:
                        w = jnp.where(tile_mask(t, live), w, 0.0)
                    ds = (w * (dot_nt(kv_buf[buf, span, HD:], da) - row_dot)).astype(BF16)
                    acc[span, :HD] += dot_nn(ds, q)
                    acc[span, HD:] += dot_nn(w.astype(BF16), da)
                    dq = dq + dot_nn(k_t[:, span], ds)
                dq_ref[pl.ds(row, RL), :] = spread_heads((dq * SCALE).T.astype(BF16))

            for n in range(1, NT + 1):
                pl.when(tiles == n)(functools.partial(work, n))
            return inner

        lax.fori_loop(first, last, one, 0)

        def put(ref, place):
            at = pl.ds(pl.multiple_of(place * PL, PL), PL)
            ref[at, :HD] = (acc[:, :HD] * SCALE).astype(BF16)
            ref[at, HD:] = acc[:, HD:].astype(BF16)

        @pl.when(slot < half)
        def _():
            put(other_ref, slot)

        @pl.when(slot >= half)
        def _():
            put(mine_ref, slot - half)

        return carry

    lax.fori_loop(0, n_slots, one_slot, 0)


VMEM = pl.BlockSpec(memory_space=pltpu.VMEM)
ANY = pl.BlockSpec(memory_space=pl.ANY)
SMEM = pl.BlockSpec(memory_space=pltpu.SMEM)


def params(mib):
    return pltpu.CompilerParams(vmem_limit_bytes=mib * MIB)


def attention_fwd(slots, lives, q, k, v, kv_arrays, offsets):
    count = q.shape[0] // RL
    return pl.pallas_call(
        functools.partial(fwd_kernel, count, offsets),
        out_shape=(
            jax.ShapeDtypeStruct(q.shape, BF16),
            jax.ShapeDtypeStruct((count * 8, ROWS), F32),
        ),
        in_specs=[SMEM] * 2 + [VMEM] * 3 + [ANY] * len(kv_arrays),
        out_specs=(VMEM, VMEM),
        scratch_shapes=[pltpu.VMEM((2, PL, 2 * HD), BF16), pltpu.SemaphoreType.DMA((2,))],
        compiler_params=params(24),
        cost_estimate=pl.CostEstimate(
            flops=count * ROWS * PL * HD * 8, bytes_accessed=count * PL * HD * 4, transcendentals=count * ROWS * PL
        ),
        name="attention_fwd",
    )(slots, lives, q, k, v, *kv_arrays)


def attention_bwd(starts, order, lives, q, k, v, da, att, lse, kv_arrays, offsets):
    n_slots = len(offsets)
    block = jax.ShapeDtypeStruct((n_slots // 2 * PL, 2 * HD), BF16)
    share = n_slots
    return pl.pallas_call(
        functools.partial(bwd_kernel, n_slots, offsets),
        out_shape=(
            jax.ShapeDtypeStruct(q.shape, BF16),
            jax.ShapeDtypeStruct(k.shape, BF16),
            jax.ShapeDtypeStruct(v.shape, BF16),
            block,
            block,
        ),
        in_specs=[SMEM] * 3 + [VMEM] * 6 + [ANY] * len(kv_arrays),
        out_specs=(VMEM,) * 5,
        scratch_shapes=[
            pltpu.VMEM((2, PL, 2 * HD), BF16),
            pltpu.VMEM((HD, PL), BF16),
            pltpu.VMEM((PL, 2 * HD), F32),
            pltpu.SemaphoreType.DMA((2,)),
        ],
        compiler_params=params(32),
        cost_estimate=pl.CostEstimate(
            flops=share * ROWS * PL * HD * 20, bytes_accessed=share * PL * HD * 16, transcendentals=share * ROWS * PL
        ),
        name="attention_bwd",
    )(starts, order, lives, q, k, v, da, att, lse, *kv_arrays)


def grad_proj_kernel(g0, g1, g2, g3, w_own, w_other, own_ref, other_ref):
    for w_ref, out_ref in ((w_other, other_ref), (w_own, own_ref)):
        total = None
        for i, g in enumerate((g0, g1, g2, g3)):
            part = dot_nt(g[...], w_ref[:, i * 512 : (i + 1) * 512])
            total = part if total is None else total + part
        out_ref[...] = total.astype(out_ref.dtype)


def grad_proj(g0, g1, g2, g3, w_own, w_other):
    rows = g0.shape[0]
    tile = 256
    block = pl.BlockSpec((tile, 512), lambda i: (i, 0))
    whole = pl.BlockSpec((512, 2048), lambda i: (0, 0))
    return pl.pallas_call(
        grad_proj_kernel,
        grid=(rows // tile,),
        out_shape=(jax.ShapeDtypeStruct((rows, 512), F32), jax.ShapeDtypeStruct((rows, 512), BF16)),
        in_specs=[block] * 4 + [whole] * 2,
        out_specs=(block, block),
        compiler_params=params(24),
        cost_estimate=pl.CostEstimate(flops=rows * 2048 * 1024 * 2, bytes_accessed=rows * 6144 + 4 * MIB, transcendentals=0),
        name="grad_projection",
    )(g0, g1, g2, g3, w_own, w_other)


def out_proj_kernel(a_own, a_other, w_own, w_other, *outs):
    for i, out in enumerate(outs):
        span = slice(i * 512, (i + 1) * 512)
        out[...] = (dot_nn(a_own[...], w_own[:, span]) + dot_nn(a_other[...], w_other[:, span])).astype(out.dtype)


def out_proj(a_own, a_other, w_own, w_other):
    rows = a_own.shape[0]
    tile = 256
    block = pl.BlockSpec((tile, 512), lambda i: (i, 0))
    whole = pl.BlockSpec((512, 2048), lambda i: (0, 0))
    return pl.pallas_call(
        out_proj_kernel,
        grid=(rows // tile,),
        out_shape=(jax.ShapeDtypeStruct((rows, 512), BF16),) * 4,
        in_specs=[block] * 2 + [whole] * 2,
        out_specs=(block,) * 4,
        compiler_params=params(24),
        cost_estimate=pl.CostEstimate(flops=rows * 2048 * 1024 * 2, bytes_accessed=rows * 6144 + 4 * MIB, transcendentals=0),
        name="out_projection",
    )(a_own, a_other, w_own, w_other)


def add(*arrays):
    return functools.reduce(lambda a, b: a + b, [a.astype(F32) for a in arrays]).astype(BF16)


def body(
    queries,
    resp_keys,
    resp_values,
    prompt_keys,
    prompt_values,
    out_weight,
    grad_out,
    response_group,
    prompt_len,
):
    kv_at, seq_at = lax.axis_index("kv"), lax.axis_index("seq")
    x, z_lo = kv_at // 2, kv_at % 2
    z_hi, y, core = seq_at // 8, (seq_at // 2) % 4, seq_at % 2
    n_resp = response_group.shape[0]

    groups = response_group[:, 0]
    place = jnp.array(PLACE, jnp.int32)
    rel = ((groups // 8) ^ z_hi) * 4 + (groups // 2 - y) % 4
    rel_hot = rel[:, None] == jnp.arange(8, dtype=jnp.int32)[None, :]
    index = jnp.sum(jnp.where(rel_hot, place[None, :], 0), axis=1)
    other_core = (groups % 2) ^ core
    slots = index + 8 * other_core
    member = groups[:, None] == jnp.arange(16, dtype=jnp.int32)[None, :]
    lives = jnp.sum(jnp.where(member, prompt_len[None, :], 0), axis=1)
    rank_of = [0] * 16
    rank = 0
    stage_ranks = []
    for stage in STAGES:
        stage_ranks.append((rank, rank + 2 * len(stage)))
        for extra in (8, 0):
            for i in stage:
                rank_of[i + extra] = rank
                rank += 1
    rank_table = jnp.array(rank_of, jnp.int32)
    slot_hot = slots[:, None] == jnp.arange(16, dtype=jnp.int32)[None, :]
    ranks = jnp.sum(jnp.where(slot_hot, rank_table[None, :], 0), axis=1)
    sort_key = ranks * 16 + jnp.arange(n_resp, dtype=jnp.int32)
    position = jnp.sum((sort_key[None, :] < sort_key[:, None]).astype(jnp.int32), axis=1)
    placed = position[None, :] == jnp.arange(n_resp, dtype=jnp.int32)[:, None]
    order = jnp.sum(jnp.where(placed, jnp.arange(n_resp, dtype=jnp.int32)[None, :], 0), axis=1)
    lives_sorted = jnp.sum(jnp.where(placed, lives[None, :], 0), axis=1)
    starts = jnp.sum((ranks[None, :] < jnp.arange(17, dtype=jnp.int32)[:, None]).astype(jnp.int32), axis=1)

    g0 = grad_out
    g3 = kv_send(g0, X_UP)
    g1 = kv_send(g0, X_DOWN)
    kv_own = jnp.concatenate([prompt_keys, prompt_values], axis=1)
    p = [None] * 8
    p[A0] = kv_own
    p[B0] = seq_send(kv_own, Z_HI)
    p[AM] = seq_send(kv_own, Y_UP)
    p[AP] = seq_send(kv_own, Y_DOWN)

    def weight_cols(rows, lo):
        parts = []
        for k in range(4):
            col = ((x + k) % 4 * 2 + lo) * 512
            parts.append(lax.dynamic_slice(rows, (0, col), (rows.shape[0], 512)))
        return jnp.concatenate(parts, axis=1)

    give = weight_cols(lax.dynamic_slice(out_weight, (core * 256, 0), (256, 4096)), 1 - z_lo)
    got_a = kv_send(give, Z_LO)
    w_own = weight_cols(out_weight, z_lo)
    p[BM] = seq_send(p[B0], Y_UP)
    p[BP] = seq_send(p[B0], Y_DOWN)
    g2_a = kv_send(g3[:512], X_UP)
    g2_b = kv_send(g1[512:], X_DOWN)
    p[A2] = seq_send(p[AM], Y_UP)
    p[B2] = seq_send(p[BP], Y_DOWN)
    got_b = seq_send(got_a, CORE)
    w_other = jnp.where(
        core == 0, jnp.concatenate([got_a, got_b], axis=0), jnp.concatenate([got_b, got_a], axis=0)
    )
    swap1 = seq_send(jnp.concatenate([p[A0], p[B0], p[AM], p[AP]], axis=0), CORE)
    swap2 = seq_send(jnp.concatenate([p[BM], p[BP], p[A2]], axis=0), CORE)
    swap3 = seq_send(p[B2], CORE)
    where_is = {i: (p[i], 0) for i in range(8)}
    for n, i in enumerate((A0, B0, AM, AP)):
        where_is[8 + i] = (swap1, n * PL)
    for n, i in enumerate((BM, BP, A2)):
        where_is[8 + i] = (swap2, n * PL)
    where_is[8 + B2] = (swap3, 0)

    def sources(wanted):
        arrays, offsets = [], []
        for slot in wanted:
            array, off = where_is[slot]
            known = [i for i, a in enumerate(arrays) if a is array]
            if not known:
                arrays.append(array)
                known = [len(arrays) - 1]
            offsets.append((known[0], off))
        return arrays, offsets

    da_parts = []
    for lo, g2 in ((0, g2_a), (512, g2_b)):
        mine, other = grad_proj(g0[lo : lo + 512], g1[lo : lo + 512], g2, g3[lo : lo + 512], w_own, w_other)
        da_parts.append((mine, kv_send(other, Z_LO)))
    da = jnp.concatenate([add(a, b) for a, b in da_parts], axis=0)

    all_arrays, all_offsets = sources(range(16))
    att_parts, lse_parts = [], []
    for lo in (0, HALF):
        span = slice(lo * RL, (lo + HALF) * RL)
        att, lse = attention_fwd(
            slots[lo : lo + HALF], lives[lo : lo + HALF],
            queries[span], resp_keys[span], resp_values[span], all_arrays, all_offsets,
        )
        att_parts.append(att)
        lse_parts.append(lse)
    outs = []
    for half, att in enumerate(att_parts):
        o0, o1, o2, o3 = out_proj(att, kv_send(att, Z_LO), w_own, w_other)
        if half == 0:
            far = kv_send(o2, X_UP)
            from_up = kv_send(o3, X_DOWN)
            from_down = kv_send(add(o1, far), X_UP)
        else:
            far = kv_send(o2, X_DOWN)
            from_down = kv_send(o1, X_UP)
            from_up = kv_send(add(o3, far), X_DOWN)
        outs.append(add(o0, from_up, from_down))
    layer_out = jnp.concatenate(outs, axis=0)

    att = jnp.concatenate(att_parts, axis=0)
    lse = jnp.concatenate(lse_parts, axis=0)
    own_grads, sums = [], {}
    for stage, (lo, hi) in zip(STAGES, stage_ranks):
        arrays, offsets = sources([i + 8 for i in stage] + list(stage))
        dq, dk, dv, other, mine = attention_bwd(
            starts[lo : hi + 1], order, lives_sorted,
            queries, resp_keys, resp_values, da, att, lse, arrays, offsets,
        )
        own_grads.append((dq, dk, dv))
        got = seq_send(other, CORE)
        for n, i in enumerate(stage):
            sums[i] = (mine[n * PL : (n + 1) * PL], got[n * PL : (n + 1) * PL])
        if A2 in stage:
            far_a = seq_send(add(*sums[A2]), Y_UP)
            far_b = seq_send(add(*sums[B2]), Y_DOWN)
        elif AM in stage:
            b_down = seq_send(add(*sums[BP]), Y_UP)
            a_up = seq_send(add(*sums[AM]), Y_DOWN)
            a_down = seq_send(add(*sums[AP], far_a), Y_UP)
            b_up = seq_send(add(*sums[BM], far_b), Y_DOWN)
        else:
            from_hi = seq_send(add(*sums[B0], b_down, b_up), Z_HI)
            prompt_grad = add(*sums[A0], a_down, a_up, from_hi)

    stage_of = (ranks >= stage_ranks[1][0]).astype(jnp.int32) + (ranks >= stage_ranks[2][0]).astype(jnp.int32)

    def pick(parts):
        width = parts[0].shape[1]
        at = stage_of[:, None, None]
        cut = [a.reshape(n_resp, RL, width) for a in parts]
        return jnp.where(at == 0, cut[0], jnp.where(at == 1, cut[1], cut[2])).reshape(n_resp * RL, width)

    query_grad, key_grad, value_grad = (pick(parts) for parts in zip(*own_grads))
    return (layer_out, query_grad, key_grad, value_grad, prompt_grad[:, :HD], prompt_grad[:, HD:])


def solution(mesh):
    return jax.shard_map(
        body,
        mesh=mesh,
        in_specs=(
            P("seq", "kv"),
            P("seq", "kv"),
            P("seq", "kv"),
            P("seq", "kv"),
            P("seq", "kv"),
            P("kv", None),
            P("seq", "kv"),
            P("seq", None),
            P(),
        ),
        out_specs=(
            P("seq", "kv"),
            P("seq", "kv"),
            P("seq", "kv"),
            P("seq", "kv"),
            P("seq", "kv"),
            P("seq", "kv"),
        ),
        check_vma=False,
    )
```

```python
import functools
import math

import jax
import jax.numpy as jnp
from jax import lax
from jax.experimental import pallas as pl
from jax.experimental.pallas import tpu as pltpu
from jax.sharding import PartitionSpec as P

HD = 128
QPK = 4
PL = 1024
RL = 64
ROWS = QPK * RL
TILE = 256
NT = PL // TILE
SCALE = HD ** (-0.5)
LOG2E = math.log2(math.e)
C2 = SCALE * LOG2E
MIB = 1024 * 1024
F32 = jnp.float32
BF16 = jnp.bfloat16

SIDE = 8
KV_BUFS = 3


def kv_perm(move):
    return [
        (x * 2 + z, (move(x, z)[0] % 4) * 2 + move(x, z)[1]) for x in range(4) for z in range(2)
    ]


def seq_perm(move):
    pairs = []
    for h in range(2):
        for y in range(4):
            for c in range(2):
                h2, y2, c2 = move(h, y, c)
                pairs.append((h * 8 + y * 2 + c, h2 * 8 + (y2 % 4) * 2 + c2))
    return pairs


X_UP = kv_perm(lambda x, z: (x + 1, z))
X_DOWN = kv_perm(lambda x, z: (x - 1, z))
Z_LO = kv_perm(lambda x, z: (x, 1 - z))
Z_HI = seq_perm(lambda h, y, c: (1 - h, y, c))
CORE = seq_perm(lambda h, y, c: (h, y, 1 - c))
SIDE_GROUPS = [[h * SIDE + i for i in range(SIDE)] for h in range(2)]
Y_UP = seq_perm(lambda h, y, c: (h, y + 1, c))
Y_DOWN = seq_perm(lambda h, y, c: (h, y - 1, c))


def kv_send(a, perm):
    return lax.ppermute(a, "kv", perm)


def seq_send(a, perm):
    return lax.ppermute(a, "seq", perm)


def dot_nt(a, b):
    return lax.dot_general(a, b, (((1,), (1,)), ((), ())), preferred_element_type=F32)


def dot_nn(a, b):
    return lax.dot_general(a, b, (((1,), (0,)), ((), ())), preferred_element_type=F32)


def dot_tn(a, b):
    return lax.dot_general(a, b, (((0,), (0,)), ((), ())), preferred_element_type=F32)


def stacked_heads(block):
    return jnp.concatenate([block[:, h * HD : (h + 1) * HD] for h in range(QPK)], axis=0)


def spread_heads(stacked):
    return jnp.concatenate([stacked[h * RL : (h + 1) * RL] for h in range(QPK)], axis=1)


def causal_mask():
    key = lax.broadcasted_iota(jnp.int32, (RL, ROWS), 0)
    query = lax.broadcasted_iota(jnp.int32, (RL, ROWS), 1) % RL
    return key <= query


def tile_mask(tile, live):
    key = lax.broadcasted_iota(jnp.int32, (TILE, ROWS), 0) + tile * TILE
    return key < live


ANY = pl.BlockSpec(memory_space=pl.ANY)
SMEM = pl.BlockSpec(memory_space=pltpu.SMEM)
VMEM = pl.BlockSpec(memory_space=pltpu.VMEM)


def work_of(us):
    return pl.CostEstimate(flops=int(us * 1.15e9), bytes_accessed=int(us * 1e5), transcendentals=0)


def run(kernel, scalars, near, far, after, outs, scratch, mib, name, cost, out_specs=None, aliases=None):
    n_in, n_after = len(scalars) + len(near) + len(far), len(after)

    def entry(*refs):
        kernel(*refs[:n_in], *refs[n_in + n_after :])

    return pl.pallas_call(
        entry,
        out_shape=tuple(outs),
        in_specs=[SMEM] * len(scalars) + [VMEM] * len(near) + [ANY] * (len(far) + n_after),
        out_specs=out_specs or (ANY,) * len(outs),
        scratch_shapes=scratch,
        input_output_aliases=aliases or {},
        compiler_params=pltpu.CompilerParams(vmem_limit_bytes=mib * MIB),
        cost_estimate=work_of(cost),
        name=name,
    )(*scalars, *near, *far, *after)


def copy_all(pairs, sems, rows=256):
    for i, (src, dst) in enumerate(pairs):
        for lo in range(0, src.shape[0], rows):
            piece = pl.ds(lo, min(rows, src.shape[0]))
            pltpu.make_async_copy(src.at[piece], dst.at[piece], sems.at[i]).start()
    return [pltpu.make_async_copy(src, dst, sems.at[i]) for i, (src, dst) in enumerate(pairs)]


def place_of(at, slot):
    return lax.rem(at[3] + lax.rem(slot, 4), 4) * 2 + (at[2] ^ (1 - slot // 4))


def prompt_rows(place):
    return pl.ds(pl.multiple_of(place * PL, PL), PL)


def start_slot(at, kv_in, starts, slot, last, kv_buf, sem):
    known = lax.min(slot, last - 1)

    @pl.when((slot < last) & (starts[known + 1] > starts[known]))
    def _():
        buf = lax.rem(slot, KV_BUFS)
        pltpu.make_async_copy(kv_in.at[prompt_rows(place_of(at, slot))], kv_buf.at[buf], sem.at[buf]).start()


def wait_slot(kv_in, buf, kv_buf, sem):
    pltpu.make_async_copy(kv_in.at[pl.ds(0, PL)], kv_buf.at[buf], sem.at[buf]).wait()


def per_response(order, lives, starts, slot, work):
    def one(p, carry):
        r = order[p]
        live = lives[p]
        tiles = (live + TILE - 1) // TILE
        row = pl.ds(pl.multiple_of(r * RL, RL), RL)
        for n in range(1, NT + 1):
            pl.when(tiles == n)(functools.partial(work, r, row, live, n))
        return carry

    lax.fori_loop(starts[slot], starts[slot + 1], one, 0)


def lse_rows(r):
    return pl.ds(pl.multiple_of(r * 8, 8), 8)


def load_all(pairs, sems):
    for c in copy_all(pairs, sems, 256):
        c.wait()


def fwd_kernel(at, starts, order, lives, q_in, k_in, v_in, *rest):
    kv_in, att_ref, lse_ref, q_ref, k_ref, v_ref, kv_buf, kv_sem, in_sem = rest[-9:]
    earlier = rest[:-9]
    for i in range(KV_BUFS - 1):
        start_slot(at, kv_in, starts, i, SIDE, kv_buf, kv_sem)
    local = ((q_in, q_ref), (k_in, k_ref), (v_in, v_ref))
    for c in copy_all([*local, *zip(earlier, (att_ref, lse_ref))], in_sem, 128):
        c.wait()

    def one_slot(slot, carry):
        kv = lax.rem(slot, KV_BUFS)
        start_slot(at, kv_in, starts, slot + KV_BUFS - 1, SIDE, kv_buf, kv_sem)

        @pl.when(starts[slot + 1] > starts[slot])
        def _():
            wait_slot(kv_in, kv, kv_buf, kv_sem)

        def work(r, row, live, n):
            q = stacked_heads(q_ref[row, :])
            scores = [dot_nt(kv_buf[kv, t * TILE : (t + 1) * TILE, :HD], q) for t in range(n)]
            scores[-1] = jnp.where(tile_mask(n - 1, live), scores[-1], -jnp.inf)
            own = jnp.where(causal_mask(), dot_nt(k_ref[row, :], q), -jnp.inf)
            top = jnp.max(own, axis=0, keepdims=True)
            for s in scores:
                top = jnp.maximum(top, jnp.max(s, axis=0, keepdims=True))
            top = top * C2
            w_own = jnp.exp2(own * C2 - top)
            total = jnp.sum(w_own, axis=0, keepdims=True)
            out = dot_tn(v_ref[row, :], w_own.astype(BF16))
            for t, s in enumerate(scores):
                w = jnp.exp2(s * C2 - top)
                total = total + jnp.sum(w, axis=0, keepdims=True)
                out = out + dot_tn(kv_buf[kv, t * TILE : (t + 1) * TILE, HD:], w.astype(BF16))
            out = out * (1.0 / total)
            att_ref[row, :] = spread_heads(out.T.astype(BF16))
            lse_ref[lse_rows(r), :] = jnp.broadcast_to(top + jnp.log2(total), (8, ROWS))

        per_response(order, lives, starts, slot, work)
        return carry

    lax.fori_loop(0, SIDE, one_slot, 0)


def bwd_kernel(slots, whole, at, starts, order, lives, *refs):
    ins, (dq_ref, dk_ref, dv_ref, sum_ref), scratch = refs[: -4 - 16], refs[-4 - 16 : -16], refs[-16:]
    q_in, k_in, v_in, att_in, lse_in, own_in, got_in, kv_in, *earlier = ins
    q_ref, k_ref, v_ref, att_ref, lse_ref, own_s, got_s, dq_s, dk_s, dv_s, kv_buf, k_t, acc, blk_s, kv_sem, in_sem = scratch
    first, last = slots
    for i in range(first, first + KV_BUFS - 1):
        start_slot(at, kv_in, starts, i, last, kv_buf, kv_sem)
    local = (
        (q_in, q_ref), (k_in, k_ref), (v_in, v_ref), (att_in, att_ref), (lse_in, lse_ref), (own_in, own_s),
        (got_in, got_s),
    )
    for c in copy_all([*local, *zip(earlier, (dq_s, dk_s, dv_s))], in_sem, 256):
        c.wait()

    def put(slot):
        blk = lax.rem(slot, 2)
        place = place_of(at, slot) if whole else slot - first
        return pltpu.make_async_copy(blk_s.at[blk], sum_ref.at[prompt_rows(place)], in_sem.at[blk])

    def one_slot(slot, carry):
        kv = lax.rem(slot, KV_BUFS)
        start_slot(at, kv_in, starts, slot + KV_BUFS - 1, last, kv_buf, kv_sem)
        acc[...] = jnp.zeros_like(acc)

        @pl.when(starts[slot + 1] > starts[slot])
        def _():
            wait_slot(kv_in, kv, kv_buf, kv_sem)
            k_t[...] = kv_buf[kv, :, :HD].T

        def work(r, row, live, n):
            q = stacked_heads(q_ref[row, :])
            got = got_s[row, :]
            low, high = got[:, : 2 * HD], got[:, 2 * HD :]
            got = jnp.concatenate([jnp.where(at[2] == 0, low, high), jnp.where(at[2] == 0, high, low)], axis=1)
            da = (stacked_heads(own_s[row, :]).astype(F32) + stacked_heads(got).astype(F32)).astype(BF16)
            prod = da.astype(F32) * stacked_heads(att_ref[row, :]).astype(F32)
            near = prod.astype(BF16)
            rest_of = (prod - near.astype(F32)).astype(BF16)
            ones = jnp.ones((8, HD), BF16)
            row_dot = (dot_nt(ones, near) + dot_nt(ones, rest_of))[:1]
            lse = lse_ref[lse_rows(r), :][:1]
            k_own = k_ref[row, :]
            w = jnp.exp2(dot_nt(k_own, q) * C2 - lse)
            w = jnp.where(causal_mask(), w, 0.0)
            ds = (w * (dot_nt(v_ref[row, :], da) - row_dot)).astype(BF16)
            dk_s[row, :] = (dot_nn(ds, q) * SCALE).astype(BF16)
            dv_s[row, :] = dot_nn(w.astype(BF16), da).astype(BF16)
            dq = dot_tn(k_own, ds)
            for t in range(n):
                span = slice(t * TILE, (t + 1) * TILE)
                s = dot_nt(kv_buf[kv, span, :HD], q)
                w = jnp.exp2(s * C2 - lse)
                if t == n - 1:
                    w = jnp.where(tile_mask(t, live), w, 0.0)
                ds = (w * (dot_nt(kv_buf[kv, span, HD:], da) - row_dot)).astype(BF16)
                acc[span, :HD] += dot_nn(ds, q)
                acc[span, HD:] += dot_nn(w.astype(BF16), da)
                dq = dq + dot_nn(k_t[:, span], ds)
            dq_s[row, :] = spread_heads((dq * SCALE).T.astype(BF16))

        per_response(order, lives, starts, slot, work)

        @pl.when(slot >= first + 2)
        def _():
            put(slot - 2).wait()

        blk = lax.rem(slot, 2)
        blk_s[blk, :, :HD] = (acc[:, :HD] * SCALE).astype(BF16)
        blk_s[blk, :, HD:] = acc[:, HD:].astype(BF16)
        put(slot).start()
        return carry

    lax.fori_loop(first, last, one_slot, 0)
    put(jnp.int32(last - 2)).wait()
    put(jnp.int32(last - 1)).wait()
    for c in copy_all(((dq_s, dq_ref), (dk_s, dk_ref), (dv_s, dv_ref)), in_sem, 256):
        c.wait()


def shape(*dims, dtype=BF16):
    return jax.ShapeDtypeStruct(dims, dtype)


def attention_fwd(at, starts, order, lives, q, k, v, kv, earlier, after):
    return run(
        fwd_kernel,
        (at, starts, order, lives),
        (),
        (q, k, v, *earlier, kv),
        after,
        (shape(*q.shape), shape(q.shape[0] // RL * 8, ROWS, dtype=F32)),
        [
            pltpu.VMEM(q.shape, BF16),
            pltpu.VMEM(k.shape, BF16),
            pltpu.VMEM(v.shape, BF16),
            pltpu.VMEM((KV_BUFS, PL, 2 * HD), BF16),
            pltpu.SemaphoreType.DMA((KV_BUFS,)),
            pltpu.SemaphoreType.DMA((5,)),
        ],
        56,
        "attention_fwd",
        300,
        (VMEM, VMEM),
    )


def attention_bwd(slots, cost, at, starts, order, lives, q, k, v, att, lse, own, got, kv, earlier, after):
    whole = slots == (0, SIDE)
    return run(
        functools.partial(bwd_kernel, slots, whole),
        (at, starts, order, lives),
        (),
        (q, k, v, att, lse, own, got, kv, *earlier),
        after,
        (shape(*q.shape), shape(*k.shape), shape(*v.shape), shape((slots[1] - slots[0]) * PL, 2 * HD)),
        [
            pltpu.VMEM(q.shape, BF16),
            pltpu.VMEM(k.shape, BF16),
            pltpu.VMEM(v.shape, BF16),
            pltpu.VMEM(q.shape, BF16),
            pltpu.VMEM(lse.shape, F32),
            pltpu.VMEM(q.shape, BF16),
            pltpu.VMEM(q.shape, BF16),
            pltpu.VMEM(q.shape, BF16),
            pltpu.VMEM(k.shape, BF16),
            pltpu.VMEM(v.shape, BF16),
            pltpu.VMEM((KV_BUFS, PL, 2 * HD), BF16),
            pltpu.VMEM((HD, PL), BF16),
            pltpu.VMEM((PL, 2 * HD), F32),
            pltpu.VMEM((2, PL, 2 * HD), BF16),
            pltpu.SemaphoreType.DMA((KV_BUFS,)),
            pltpu.SemaphoreType.DMA((10,)),
        ],
        56,
        "attention_bwd",
        cost,
    )


def weight_column(at, k, z_lo):
    return pl.multiple_of((lax.rem(at[0] + k, 4) * 2 + z_lo) * 512, 512)


def hold(a, after):
    def kernel(a_ref, out):
        pass

    return run(kernel, (), (), (a,), after, (shape(*a.shape),), [], 4, "hold", 0.2, aliases={0: 0})[0]


def pack_prompts(k, v):
    def kernel(k_ref, v_ref, kv_out, kv_s, sems):
        loads = copy_all(((k_ref, kv_s.at[:, pl.ds(0, HD)]), (v_ref, kv_s.at[:, pl.ds(HD, HD)])), sems)
        for c in loads:
            c.wait()
        for c in copy_all(((kv_s, kv_out),), sems):
            c.wait()

    wide = (k.shape[0], 2 * HD)
    return run(
        kernel, (), (), (k, v), (), (shape(*wide),), [pltpu.VMEM(wide, BF16), pltpu.SemaphoreType.DMA((2,))], 56,
        "pack_prompts", 2,
    )[0]


def pack_weight(at, weight, after):
    def kernel(at, w_ref, own, give, own_s, give_s, sems):
        rows = pl.ds(pl.multiple_of(at[2] * 256, 256), 256)
        pairs = []
        for k in range(4):
            cols = pl.ds(k * 512, 512)
            pairs.append((w_ref.at[rows, pl.ds(weight_column(at, k, 1 - at[1]), 512)], give_s.at[:, cols]))
            pairs.append((w_ref.at[:, pl.ds(weight_column(at, k, at[1]), 512)], own_s.at[:, cols]))
        loads = copy_all(pairs, sems)
        for c in loads[0::2]:
            c.wait()
        last = copy_all(((give_s, give),), sems, 64)
        for c in loads[1::2]:
            c.wait()
        for c in last + copy_all(((own_s, own),), sems.at[pl.ds(1, 1)], 128):
            c.wait()

    return run(
        kernel, (at,), (), (weight,), after, (shape(512, 2048), shape(256, 2048)),
        [pltpu.VMEM((512, 2048), BF16), pltpu.VMEM((256, 2048), BF16), pltpu.SemaphoreType.DMA((8,))], 48,
        "pack_weight", 3,
    )


TOKENS = 256


def weight_specs():
    parts = []
    for rows in (512, 256, 256):
        for k in range(4):
            parts.append(pl.BlockSpec((rows, 512), functools.partial(lambda k, i: (0, k), k)))
    return parts


def token_spec(index=lambda i: i):
    return pl.BlockSpec((TOKENS, 512), lambda i: (index(i), 0))


def project(kernel, name, at, arrays, specs, weights, n_out, rows):
    w_own, got_a, got_b = weights
    return pl.pallas_call(
        kernel,
        grid=(rows // TOKENS,),
        out_shape=(shape(rows, 512),) * n_out,
        in_specs=[SMEM, *specs, *weight_specs()],
        out_specs=(token_spec(),) * n_out,
        compiler_params=pltpu.CompilerParams(vmem_limit_bytes=56 * MIB),
        cost_estimate=work_of(0.01),
        name=name,
    )(at, *arrays, *[w_own] * 4, *[got_a] * 4, *[got_b] * 4)


def grad_proj(at, weights, g0, g1, g2_low, g2_high, g3):
    rows = g0.shape[0]
    cut = rows // 2 // TOKENS

    def kernel(at, g0, g1, g2_low, g2_high, g3, *refs):
        w_own, w_a, w_b, (own_ref, other_ref) = refs[:4], refs[4:8], refs[8:12], refs[12:]
        g2 = jnp.where(pl.program_id(0) < cut, g2_low[...], g2_high[...])
        tokens = (g0[...], g1[...], g2, g3[...])
        for w, out, cols in ((w_a, other_ref, slice(0, 256)), (w_b, other_ref, slice(256, 512)), (w_own, own_ref, slice(0, 512))):
            total = None
            for k in range(4):
                part = dot_nt(tokens[k], w[k][...])
                total = part if total is None else total + part
            out[:, cols] = total.astype(BF16)

    low, high = token_spec(lambda i: jnp.minimum(i, cut - 1)), token_spec(lambda i: jnp.maximum(i - cut, 0))
    specs = [token_spec(), token_spec(), low, high, token_spec()]
    return project(kernel, "grad_projection", at, (g0, g1, g2_low, g2_high, g3), specs, weights, 2, rows)


def out_proj(at, weights, att, att_other):
    def kernel(at, att, other, *refs):
        w_own, w_a, w_b, outs = refs[:4], refs[4:8], refs[8:12], refs[12:]
        halves = [other[:, pl.ds(pl.multiple_of(lax.rem(at[2] + i, 2) * 256, 256), 256)] for i in range(2)]
        for k in (2, 3, 1, 0):
            total = dot_nn(att[...], w_own[k][...]) + dot_nn(halves[0], w_a[k][...]) + dot_nn(halves[1], w_b[k][...])
            outs[k][...] = total.astype(BF16)

    specs = [token_spec(), token_spec()]
    return project(kernel, "out_projection", at, (att, att_other), specs, weights, 4, att.shape[0])


def add(*arrays):
    return functools.reduce(lambda a, b: a + b, [a.astype(F32) for a in arrays]).astype(BF16)


def body(
    queries,
    resp_keys,
    resp_values,
    prompt_keys,
    prompt_values,
    out_weight,
    grad_out,
    response_group,
    prompt_len,
):
    kv_at, seq_at = lax.axis_index("kv"), lax.axis_index("seq")
    x, z_lo = kv_at // 2, kv_at % 2
    z_hi, y, core = seq_at // SIDE, (seq_at // 2) % 4, seq_at % 2
    n_resp = response_group.shape[0]

    groups = response_group[:, 0]
    count = jnp.arange(n_resp, dtype=jnp.int32)
    member = groups[:, None] == jnp.arange(2 * SIDE, dtype=jnp.int32)[None, :]
    lives = jnp.sum(jnp.where(member, prompt_len[None, :], 0), axis=1)
    slots = (groups % 2 == core) * 4 + (groups % SIDE // 2 - y) % 4
    ranks = slots + jnp.where(groups // SIDE == z_hi, SIDE, 0)
    sort_key = ranks * n_resp + count
    position = jnp.sum((sort_key[None, :] < sort_key[:, None]).astype(jnp.int32), axis=1)
    placed = position[None, :] == count[:, None]
    order = jnp.sum(jnp.where(placed, count[None, :], 0), axis=1)
    lives_sorted = jnp.sum(jnp.where(placed, lives[None, :], 0), axis=1)
    bounds = jnp.arange(2 * SIDE + 1, dtype=jnp.int32)
    starts = jnp.sum((ranks[None, :] < bounds[:, None]).astype(jnp.int32), axis=1)
    at = jnp.stack([x, z_lo, core, y]).astype(jnp.int32)

    def spread(a):
        return lax.all_gather(a, "seq", axis=0, tiled=True, axis_index_groups=SIDE_GROUPS)

    cut = grad_out.shape[0] // 2
    local = (queries, resp_keys, resp_values)
    responses = (order, lives_sorted, *local)
    kv_own = pack_prompts(prompt_keys, prompt_values)
    kv_near = spread(kv_own)
    kv_other = seq_send(kv_own, Z_HI)
    g3, g1 = kv_send(grad_out, X_UP), kv_send(grad_out, X_DOWN)
    w_own, give = pack_weight(at, out_weight, (kv_own,))
    got_a = kv_send(give, Z_LO)
    g2_low, g2_high = kv_send(g3[:cut], X_UP), kv_send(g1[cut:], X_DOWN)
    got_b = seq_send(got_a, CORE)
    weights = (w_own, got_a, got_b)

    far_starts, near_starts = starts[: SIDE + 1], starts[SIDE:]
    first = attention_fwd(at, near_starts, *responses, kv_near, (), ())
    kv_far = spread(hold(kv_other, (first[1], g2_low, g2_high, got_a)))
    own, other = grad_proj(at, weights, grad_out, g1, hold(g2_low, (first[1],)), g2_high, g3)
    da = (own, kv_send(other, Z_LO))
    att, lse = attention_fwd(at, far_starts, *responses, kv_far, first, (other,))
    att_other = kv_send(att, Z_LO)

    heads = (*responses, att, lse, *da)
    half = SIDE // 2
    *grads, part = attention_bwd((0, SIDE), 15, at, far_starts, *heads, kv_far, (), ())
    from_hi = seq_send(
        lax.psum_scatter(part, "seq", scatter_dimension=0, tiled=True, axis_index_groups=SIDE_GROUPS), Z_HI
    )
    *grads, part = attention_bwd((0, half), 0.01, at, near_starts, *heads, kv_near, grads, (part,))
    got = seq_send(part, CORE)
    o0, o1, o2, o3 = out_proj(at, weights, att, hold(att_other, (part,)))
    far_up, far_down = kv_send(o2[:cut], X_UP), kv_send(o2[cut:], X_DOWN)
    *grads, mine = attention_bwd((half, SIDE), 300, at, near_starts, *heads, kv_near, grads, (o3,))

    def block(n, lo, hi):
        rows = slice(n * PL + lo, n * PL + hi)
        return mine[rows].astype(F32) + got[rows].astype(F32)

    mid = PL // 2
    y_up = seq_send(hold(block(2, 0, mid).astype(BF16), (far_up, far_down)), Y_UP)
    y_down = seq_send(block(2, mid, PL).astype(BF16), Y_DOWN)
    x_down = kv_send(jnp.concatenate([add(o1[:cut], far_up), o1[cut:]], axis=0), X_UP)
    x_up = kv_send(jnp.concatenate([o3[:cut], add(o3[cut:], far_down)], axis=0), X_DOWN)
    from_down = seq_send(jnp.concatenate([add(block(1, 0, mid), y_up), block(1, mid, PL).astype(BF16)], axis=0), Y_UP)
    from_up = seq_send(jnp.concatenate([block(3, 0, mid).astype(BF16), add(block(3, mid, PL), y_down)], axis=0), Y_DOWN)
    layer_out = add(o0, x_up, x_down)
    prompt_grad = add(block(0, 0, PL), from_up, from_down, from_hi)
    return (layer_out, *grads, prompt_grad[:, :HD], prompt_grad[:, HD:])


def solution(mesh):
    return jax.shard_map(
        body,
        mesh=mesh,
        in_specs=(
            P("seq", "kv"),
            P("seq", "kv"),
            P("seq", "kv"),
            P("seq", "kv"),
            P("seq", "kv"),
            P("kv", None),
            P("seq", "kv"),
            P("seq", None),
            P(),
        ),
        out_specs=(
            P("seq", "kv"),
            P("seq", "kv"),
            P("seq", "kv"),
            P("seq", "kv"),
            P("seq", "kv"),
            P("seq", "kv"),
        ),
        check_vma=False,
    )
```
